512 devices in a mesh: pipe: 64 (over z, y_hi, core), tensor: 8 (over y_lo, x).
Axes of the slice: x: 4, y: 8 (y_hi: 4, y_lo: 2; y = y_hi * 2 + y_lo), z: 8, core: 2. Of those that a mesh axis runs over, the one named last changes fastest.
Arguments:
- qkv_now: bfloat16 [64, 3, 128, 6144], P('pipe', None, None, 'tensor'), may hold values from -150 to 150
- held_stash: bfloat16 [64, 2, 3, 128, 6144], P('pipe', None, None, None, 'tensor'), may hold values from -150 to 150
- cotangent: bfloat16 [64, 128, 6144], P('pipe', None, 'tensor'), may hold values from -6 to 6
- norm_gain: float32 [6144], P('tensor'), may hold values from 0.1 to 1.9
- fetch_slot: int32 [64], replicated, may hold values from 0 to 1
Outputs:
- forward_in: bfloat16 [64, 128, 6144], P('pipe', None, 'tensor')
- grads_in: bfloat16 [64, 3, 128, 6144], P('pipe', None, None, 'tensor')
- evicted: bfloat16 [64, 128, 6144], P('pipe', None, 'tensor')
The draws below stay inside these ranges and needn't reach their ends.
All inputs are finite; a program needn't handle non-finite values.
Results may differ from the reference program's by a relative error of at most 0.009.
Values may be sent and summed in bfloat16 or wider, within the bound.
A program may use at most 64 MiB of HBM per device.

```python
import jax
import jax.numpy as jnp
from jax import lax

HS = 128
HEADS = 48
TOK_DEV = 128
SLOTS = 2
SECTIONS = 64
FEATS = 6144


def make_qkv(key, lead, strength):
    key_q, key_k, key_v = jax.random.split(key, 3)
    shape = lead + (TOK_DEV, FEATS)
    queries = jnp.clip(jax.random.normal(key_q, shape, jnp.float32), -6.0, 6.0)
    keys_drawn = jnp.clip(jax.random.normal(key_k, shape, jnp.float32), -6.0, 6.0)
    values_drawn = jnp.clip(jax.random.normal(key_v, shape, jnp.float32), -6.0, 6.0)
    head_index = (jnp.arange(FEATS) // HS).astype(jnp.float32)
    values_drawn = values_drawn * 3.0 ** (head_index / max(HEADS - 1, 1))
    rows = jnp.arange(TOK_DEV)[:, None]
    active = strength > 0.0
    target_strength = jnp.maximum(strength * (1 + (rows + 2) // 32 % 3).astype(jnp.float32), 1.0)
    next_keys = jnp.roll(keys_drawn, -1, axis=-2)
    second_rows = (rows % 32 == 29) & (rows + 2 < TOK_DEV) & active
    keys_drawn = jnp.where(second_rows, next_keys * (1.0 - 1.5 / (target_strength * HS ** 0.5)), keys_drawn)
    previous_keys = jnp.roll(keys_drawn, 1, axis=-2)
    row_strength = strength * (1 + rows // 32 % 3).astype(jnp.float32)
    first_rows = (rows % 32 == 31) & active
    queries = jnp.where(first_rows, row_strength * previous_keys, queries)
    return jnp.stack([queries, keys_drawn, values_drawn], axis=-3)


def draw_qkv_now(key, part):
    key = jax.random.fold_in(key, 11)
    strength = 0.0
    return make_qkv(key, (SECTIONS,), strength).astype(jnp.bfloat16)


def draw_held_stash(key, part):
    key = jax.random.fold_in(key, 23)
    strength = 0.0
    return make_qkv(key, (SECTIONS, SLOTS), strength).astype(jnp.bfloat16)


def touch_ends(entries, own_key, least, high):
    dims = entries.shape
    spot = [jax.random.randint(jax.random.fold_in(own_key, axis), (), 0, dims[axis]) for axis in range(len(dims))]
    entries = entries.at[tuple(spot)].set(least)
    longest = dims.index(max(dims))
    spot[longest] = (spot[longest] + 1) % dims[longest]
    return entries.at[tuple(spot)].set(high)


def block_scale(rng, shape, cuts, least, high):
    level, own = 1.0, jax.random.fold_in(rng, 6)
    for dim, parts in cuts:
        draws = jnp.exp(jax.random.uniform(jax.random.fold_in(own, dim), (parts,), jnp.float32, least / len(cuts), high / len(cuts)))
        level = level * jnp.repeat(draws, shape[dim] // parts).reshape([-1 if axis == dim else 1 for axis in range(len(shape))])
    return level


def scatter_about(own_key, extent, width, bound, shards=(), held_as=jnp.bfloat16):
    values = width * jax.random.normal(own_key, extent, jnp.float32)
    if shards:
        values = values * block_scale(own_key, extent, shards, -0.22, 0.18)
    return jnp.clip(values, -bound, bound).astype(held_as)


def setup_inputs(seed: int = 0) -> dict:
    seeds = jax.random.split(jax.random.key(seed), 6)
    qkv_now = draw_qkv_now(jax.random.fold_in(seeds[5], 71), 0)
    held_stash = draw_held_stash(jax.random.fold_in(seeds[5], 71), 0)
    cotangent = scatter_about(seeds[2], (SECTIONS, TOK_DEV, FEATS), 1.0, 6.0, ((0, 64), (2, 8)))
    norm_gain = jnp.clip(1.0 + 0.18 * jax.random.normal(seeds[3], (FEATS,), jnp.float32), 0.1, 1.9)
    fetch_slot = touch_ends(jax.random.randint(seeds[4], (SECTIONS,), 0, SLOTS), jax.random.fold_in(seeds[4], 1), 0, SLOTS - 1).astype(jnp.int32)
    return dict(qkv_now=qkv_now, held_stash=held_stash, cotangent=cotangent, norm_gain=norm_gain, fetch_slot=fetch_slot)


EPS = 1e-05

def as_float(array):
    return array.astype(jnp.float32)

def attend_heads(queries, keys_in, values_in):
    rows = queries.shape[0]
    query_heads = as_float(queries).reshape(rows, HEADS, HS)
    key_heads = as_float(keys_in).reshape(rows, HEADS, HS)
    value_heads = as_float(values_in).reshape(rows, HEADS, HS)
    score_scale = HS ** (-0.5)
    scores = jnp.einsum('ihd,jhd->hij', query_heads, key_heads) * score_scale
    causal = jnp.arange(rows)[:, None] >= jnp.arange(rows)[None, :]
    masked = jnp.where(causal[None], scores, -1e+30)
    maxima = lax.optimization_barrier(jnp.max(masked, axis=-1, keepdims=True))
    expo = jnp.exp(masked - maxima)
    probabilities = expo / lax.optimization_barrier(jnp.sum(expo, axis=-1, keepdims=True))
    prob_bf16 = probabilities.astype(jnp.bfloat16)
    attended = jnp.einsum('hij,jhd->ihd', as_float(prob_bf16), value_heads)
    return (attended.reshape(rows, HEADS * HS).astype(jnp.bfloat16), probabilities, prob_bf16)

def section_step(now, back, cot, norm_gain):
    attended, unused_p, unused_b = attend_heads(now[0], now[1], now[2])
    att_f = as_float(attended)
    ratio = lax.rsqrt(lax.optimization_barrier(jnp.sum(att_f * att_f, axis=-1)) / FEATS + EPS)
    normed = (att_f * ratio[:, None] * norm_gain[None, :]).astype(jnp.bfloat16)
    back_out, probabilities, prob_bf16 = attend_heads(back[0], back[1], back[2])
    back_f = as_float(back_out)
    back_ratio = lax.rsqrt(lax.optimization_barrier(jnp.sum(back_f * back_f, axis=-1)) / FEATS + EPS)
    scaled_cot = norm_gain[None, :] * as_float(cot)
    dot_rows = lax.optimization_barrier(jnp.sum(scaled_cot * back_f, axis=-1))
    d_out = (back_ratio[:, None] * scaled_cot - back_f * (back_ratio ** 3 * dot_rows / FEATS)[:, None]).astype(jnp.bfloat16)
    rows = cot.shape[0]
    d_heads = as_float(d_out).reshape(rows, HEADS, HS)
    query_heads = as_float(back[0]).reshape(rows, HEADS, HS)
    key_heads = as_float(back[1]).reshape(rows, HEADS, HS)
    value_heads = as_float(back[2]).reshape(rows, HEADS, HS)
    d_values = jnp.einsum('hij,ihd->jhd', as_float(prob_bf16), d_heads)
    d_probs = jnp.einsum('ihd,jhd->hij', d_heads, value_heads)
    delta = lax.optimization_barrier(jnp.sum(probabilities * d_probs, axis=-1, keepdims=True))
    d_scores = (probabilities * (d_probs - delta) * HS ** (-0.5)).astype(jnp.bfloat16)
    d_queries = jnp.einsum('hij,jhd->ihd', as_float(d_scores), key_heads)
    d_keys = jnp.einsum('hij,ihd->jhd', as_float(d_scores), query_heads)
    grads = jnp.stack([d_queries.reshape(rows, FEATS), d_keys.reshape(rows, FEATS), d_values.reshape(rows, FEATS)]).astype(jnp.bfloat16)
    return (normed, attended, grads)

def reference(qkv_now, held_stash, cotangent, norm_gain, fetch_slot):
    mirrored = held_stash[::-1]
    fetched = mirrored[jnp.arange(SECTIONS), fetch_slot]

    def one_section(packed):
        return section_step(packed[0], packed[1], packed[2], norm_gain)
    normed, attended, grads = lax.map(one_section, (qkv_now, fetched, cotangent))
    forward_in = jnp.concatenate([jnp.zeros_like(normed[:1]), normed[:-1]], axis=0)
    grads_in = jnp.concatenate([grads[1:], jnp.zeros_like(grads[:1])], axis=0)
    evicted = attended[::-1]
    return (forward_in, grads_in, evicted)
```

```python
import functools

import jax
import jax.numpy as jnp
from jax import lax
from jax.experimental import pallas as pl
from jax.experimental.pallas import tpu as pltpu
from jax.sharding import PartitionSpec as P

MESH = pl.DeviceIdType.MESH
HS = 128
EPS = 1e-05
F32 = jnp.float32
BF16 = jnp.bfloat16


def dot(x, y, dims):
    return lax.dot_general(x, y, (dims, ((), ())), preferred_element_type=F32)


def softmax_rows(queries, keys, causal):
    scores = dot(queries, keys, ((1,), (1,))) * HS ** (-0.5)
    masked = jnp.where(causal, scores, -1e30)
    expo = jnp.exp(masked - jnp.max(masked, axis=-1, keepdims=True))
    return expo / jnp.sum(expo, axis=-1, keepdims=True)


def as_row(partial):
    return jnp.sum(partial.T, axis=0, keepdims=True)


def as_columns(row):
    return jnp.broadcast_to(row, (HS, row.shape[1])).T


def kernel(
    sections, members, heads, feats,
    qkv_ref, held_ref, cot_ref, gain_ref, slot_ref,
    fwd_ref, grads_ref, evict_ref,
    held_v, send_v, back_v, qkv_v, cot_v, att_v, norm_v, prob_v, pb_v, ob_v, grad_v,
    sum_v, sums_now, sums_back,
    held_sem, qkv_sem, self_sem, zero_sem, grad_sem,
    stash_send, stash_recv, cot_send, cot_recv, evict_send, evict_recv, fwd_send, fwd_recv,
    now_send, now_recv, bsum_send, bsum_recv,
):
    p = lax.axis_index("pipe")
    t = lax.axis_index("tensor")
    last = sections - 1
    mirror = last - p
    target = last - 1 - p
    has_up = p < last
    has_down = p > 0
    to_self = target == p
    paired = has_up & jnp.logical_not(to_self)

    loads = []
    for h in range(heads):
        loads.append(pltpu.make_async_copy(held_ref.at[0, :, :, :, pl.ds(h * HS, HS)], held_v.at[h], held_sem.at[h]))
        loads[h].start()
    qkv_load = pltpu.make_async_copy(qkv_ref.at[0], qkv_v, qkv_sem)
    qkv_load.start()

    barrier = pltpu.get_barrier_semaphore()

    def greet(section, member):
        pl.semaphore_signal(barrier, inc=1, device_id=(section, member), device_id_type=MESH)

    greet(mirror, t)
    pl.when(paired)(lambda: greet(target, t))
    pl.when(has_up)(lambda: greet(p + 1, t))
    pl.when(has_down)(lambda: greet(p - 1, t))
    for d in range(1, members):
        greet(p, lax.rem(t + d, members))

    def one(flag):
        return jnp.where(flag, 1, 0)

    stash = [
        pltpu.make_async_remote_copy(
            src_ref=send_v.at[h], dst_ref=back_v.at[h], send_sem=stash_send.at[h], recv_sem=stash_recv.at[h],
            device_id=(target, t), device_id_type=MESH,
        )
        for h in range(heads)
    ]
    cot_move = pltpu.make_async_remote_copy(
        src_ref=cot_ref.at[0], dst_ref=cot_v, send_sem=cot_send, recv_sem=cot_recv, device_id=(p - 1, t), device_id_type=MESH
    )
    evict_move = pltpu.make_async_remote_copy(
        src_ref=att_v, dst_ref=evict_ref.at[0], send_sem=evict_send, recv_sem=evict_recv, device_id=(mirror, t), device_id_type=MESH
    )
    fwd_move = pltpu.make_async_remote_copy(
        src_ref=norm_v, dst_ref=fwd_ref.at[0], send_sem=fwd_send, recv_sem=fwd_recv, device_id=(p + 1, t), device_id_type=MESH
    )

    def sum_moves(which, buffer, sends, recvs):
        return [
            pltpu.make_async_remote_copy(
                src_ref=sum_v.at[which], dst_ref=buffer.at[d - 1], send_sem=sends.at[d - 1], recv_sem=recvs.at[d - 1],
                device_id=(p, lax.rem(t + d, members)), device_id_type=MESH,
            )
            for d in range(1, members)
        ]

    slot = slot_ref[mirror]
    for h in range(heads):
        loads[h].wait()
        for i in range(3):
            send_v[h, i] = jnp.where(slot == 1, held_v[h, 1, i], held_v[h, 0, i])
        if h == 0:
            pl.semaphore_wait(barrier, members + one(paired) + one(has_up) + one(has_down))
        pl.when(paired)(stash[h].start)

    pl.when(has_down)(cot_move.start)

    @pl.when(to_self)
    def _():
        own = pltpu.make_async_copy(send_v, back_v, self_sem)
        own.start()
        own.wait()

    @pl.when(p == last)
    def _():
        back_v[...] = jnp.zeros_like(back_v)
        cot_v[...] = jnp.zeros_like(cot_v)

    rows = lax.broadcasted_iota(jnp.int32, (HS, HS), 0)
    causal = rows >= lax.broadcasted_iota(jnp.int32, (HS, HS), 1)
    qkv_load.wait()
    squares = jnp.zeros((HS, HS), F32)
    for h in range(heads):
        cols = pl.ds(h * HS, HS)
        probs = softmax_rows(qkv_v[0, :, cols], qkv_v[1, :, cols], causal)
        out = dot(probs.astype(BF16), qkv_v[2, :, cols], ((1,), (0,))).astype(BF16)
        att_v[:, cols] = out
        out = out.astype(F32)
        squares += out * out
    sum_v[0] = jnp.broadcast_to(as_row(squares), (8, HS))
    now_moves = sum_moves(0, sums_now, now_send, now_recv)
    for move in now_moves:
        move.start()
    for move in now_moves:
        move.wait_recv()
    total = sum_v[0, 0:1]
    for d in range(members - 1):
        total += sums_now[d, 0:1]
    ratio = as_columns(lax.rsqrt(total / feats + EPS))
    for h in range(heads):
        cols = pl.ds(h * HS, HS)
        norm_v[:, cols] = (att_v[:, cols].astype(F32) * ratio * gain_ref[:, cols]).astype(BF16)
    pl.when(has_up)(fwd_move.start)

    @pl.when(p == 0)
    def _():
        grad_v[0] = jnp.zeros_like(grad_v[0])
        zeros = pltpu.make_async_copy(grad_v.at[0], fwd_ref.at[0], zero_sem)
        zeros.start()
        zeros.wait()

    pl.when(has_up)(cot_move.wait_recv)
    squares = jnp.zeros((HS, HS), F32)
    dots = jnp.zeros((HS, HS), F32)
    for h in range(heads):
        cols = pl.ds(h * HS, HS)
        pl.when(paired)(stash[h].wait_send)
        if h == heads - 1:
            evict_move.start()
        pl.when(paired)(stash[h].wait_recv)
        probs = softmax_rows(back_v[h, 0], back_v[h, 1], causal)
        prob_v[h] = probs
        probs = probs.astype(BF16)
        pb_v[h] = probs
        out = dot(probs, back_v[h, 2], ((1,), (0,))).astype(BF16)
        ob_v[h] = out
        out = out.astype(F32)
        squares += out * out
        dots += gain_ref[:, cols] * cot_v[:, cols].astype(F32) * out
    sum_v[1] = jnp.concatenate([as_row(squares), as_row(dots), jnp.zeros((6, HS), F32)], axis=0)
    back_moves = sum_moves(1, sums_back, bsum_send, bsum_recv)
    for move in back_moves:
        move.start()
    for move in back_moves:
        move.wait_recv()
    total = sum_v[1]
    for d in range(members - 1):
        total += sums_back[d]
    back_ratio = lax.rsqrt(total[0:1] / feats + EPS)
    pull = as_columns(back_ratio**3 * total[1:2] / feats)
    back_ratio = as_columns(back_ratio)

    for h in range(heads):
        cols = pl.ds(h * HS, HS)
        scaled = gain_ref[:, cols] * cot_v[:, cols].astype(F32)
        d_out = (back_ratio * scaled - ob_v[h].astype(F32) * pull).astype(BF16)
        probs = prob_v[h]
        d_values = dot(pb_v[h], d_out, ((0,), (0,)))
        d_probs = dot(d_out, back_v[h, 2], ((1,), (1,)))
        delta = jnp.sum(probs * d_probs, axis=-1, keepdims=True)
        d_scores = (probs * (d_probs - delta) * HS ** (-0.5)).astype(BF16)
        grad_v[0, :, cols] = dot(d_scores, back_v[h, 1], ((1,), (0,))).astype(BF16)
        grad_v[1, :, cols] = dot(d_scores, back_v[h, 0], ((0,), (0,))).astype(BF16)
        grad_v[2, :, cols] = d_values.astype(BF16)
    grads_out = pltpu.make_async_copy(grad_v, grads_ref.at[0], grad_sem)
    grads_out.start()

    pl.when(has_down)(cot_move.wait_send)
    pl.when(has_up)(fwd_move.wait_send)
    pl.when(has_down)(fwd_move.wait_recv)
    for move in now_moves + back_moves:
        move.wait_send()
    grads_out.wait()
    evict_move.wait()


def shards(sections, members, qkv_now, held_stash, cotangent, norm_gain, fetch_slot):
    rows, width = cotangent.shape[1:]
    heads = width // HS
    anywhere = pl.BlockSpec(memory_space=pl.ANY)
    dma = pltpu.SemaphoreType.DMA
    return pl.pallas_call(
        functools.partial(kernel, sections, members, heads, float(width * members)),
        name="section_step",
        out_shape=(
            jax.ShapeDtypeStruct((1, rows, width), BF16),
            jax.ShapeDtypeStruct((1, 3, rows, width), BF16),
            jax.ShapeDtypeStruct((1, rows, width), BF16),
        ),
        in_specs=[
            anywhere, anywhere, anywhere,
            pl.BlockSpec(memory_space=pltpu.VMEM),
            pl.BlockSpec(memory_space=pltpu.SMEM),
        ],
        out_specs=(anywhere, anywhere, anywhere),
        scratch_shapes=[
            pltpu.VMEM((heads, 2, 3, rows, HS), BF16),
            pltpu.VMEM((heads, 3, rows, HS), BF16),
            pltpu.VMEM((heads, 3, rows, HS), BF16),
            pltpu.VMEM((3, rows, width), BF16),
            pltpu.VMEM((rows, width), BF16),
            pltpu.VMEM((rows, width), BF16),
            pltpu.VMEM((rows, width), BF16),
            pltpu.VMEM((heads, rows, rows), F32),
            pltpu.VMEM((heads, rows, rows), BF16),
            pltpu.VMEM((heads, rows, HS), BF16),
            pltpu.VMEM((3, rows, width), BF16),
            pltpu.VMEM((2, 8, rows), F32),
            pltpu.VMEM((members - 1, 8, rows), F32),
            pltpu.VMEM((members - 1, 8, rows), F32),
            dma((heads,)), dma, dma, dma, dma,
            dma((heads,)), dma((heads,)), dma, dma, dma, dma, dma, dma,
            dma((members - 1,)), dma((members - 1,)), dma((members - 1,)), dma((members - 1,)),
        ],
        compiler_params=pltpu.CompilerParams(
            collective_id=0, has_side_effects=True, vmem_limit_bytes=24 * 1024 * 1024
        ),
    )(qkv_now, held_stash, cotangent, norm_gain[None, :], fetch_slot)


def solution(mesh):
    return jax.shard_map(
        functools.partial(shards, mesh.shape["pipe"], mesh.shape["tensor"]),
        mesh=mesh,
        in_specs=(
            P("pipe", None, None, "tensor"),
            P("pipe", None, None, None, "tensor"),
            P("pipe", None, "tensor"),
            P("tensor"),
            P(),
        ),
        out_specs=(
            P("pipe", None, "tensor"),
            P("pipe", None, None, "tensor"),
            P("pipe", None, "tensor"),
        ),
        check_vma=False,
    )
```

```python
import functools

import jax
import jax.numpy as jnp
from jax import lax
from jax.experimental import pallas as pl
from jax.experimental.pallas import tpu as pltpu
from jax.sharding import PartitionSpec as P

MESH = pl.DeviceIdType.MESH
HS = 128
EPS = 1e-05
F32 = jnp.float32
BF16 = jnp.bfloat16


def dot(x, y, dims):
    return lax.dot_general(x, y, (dims, ((), ())), preferred_element_type=F32)


def softmax_rows(queries, keys, causal):
    scores = dot(queries, keys, ((1,), (1,))) * HS ** (-0.5)
    masked = jnp.where(causal, scores, -1e30)
    expo = jnp.exp(masked - jnp.max(masked, axis=-1, keepdims=True))
    return expo / jnp.sum(expo, axis=-1, keepdims=True)


def as_row(partial):
    return jnp.sum(partial.T, axis=0, keepdims=True)


def as_columns(row):
    return jnp.broadcast_to(row, (HS, row.shape[1])).T


def kernel(
    sections, members, heads, feats,
    qkv_ref, held_ref, cot_ref, gain_hbm, slot_hbm,
    fwd_ref, grads_ref, evict_ref,
    held_v, send_v, back_v, qkv_v, cot_v, att_v, norm_v, prob_v, pb_v, ob_v, grad_v,
    sum_v, sums_now, sums_back,
    gain_ref, slot_ref, gain_sem, slot_sem, held_sem, qkv_sem, self_sem, zero_sem, grad_sem,
    stash_send, stash_recv, cot_send, cot_recv, evict_send, evict_recv, fwd_send, fwd_recv,
    now_send, now_recv, bsum_send, bsum_recv,
):
    p = lax.axis_index("pipe")
    t = lax.axis_index("tensor")
    last = sections - 1
    mirror = last - p
    target = last - 1 - p
    has_up = p < last
    has_down = p > 0
    to_self = target == p
    paired = has_up & jnp.logical_not(to_self)

    slot_load = pltpu.make_async_copy(slot_hbm, slot_ref, slot_sem)
    slot_load.start()
    gain_load = pltpu.make_async_copy(gain_hbm, gain_ref, gain_sem)
    loads = []
    for h in range(heads):
        loads.append(pltpu.make_async_copy(held_ref.at[0, :, :, :, pl.ds(h * HS, HS)], held_v.at[h], held_sem.at[h]))
        loads[h].start()
    qkv_load = pltpu.make_async_copy(qkv_ref.at[0], qkv_v, qkv_sem)
    qkv_load.start()
    gain_load.start()

    barrier = pltpu.get_barrier_semaphore()

    def greet(section, member):
        pl.semaphore_signal(barrier, inc=1, device_id=(section, member), device_id_type=MESH)

    greet(mirror, t)
    pl.when(paired)(lambda: greet(target, t))
    pl.when(has_up)(lambda: greet(p + 1, t))
    pl.when(has_down)(lambda: greet(p - 1, t))
    for d in range(1, members):
        greet(p, lax.rem(t + d, members))

    def one(flag):
        return jnp.where(flag, 1, 0)

    stash = [
        pltpu.make_async_remote_copy(
            src_ref=send_v.at[h], dst_ref=back_v.at[h], send_sem=stash_send.at[h], recv_sem=stash_recv.at[h],
            device_id=(target, t), device_id_type=MESH,
        )
        for h in range(heads)
    ]
    cot_move = pltpu.make_async_remote_copy(
        src_ref=cot_ref.at[0], dst_ref=cot_v, send_sem=cot_send, recv_sem=cot_recv, device_id=(p - 1, t), device_id_type=MESH
    )
    evict_move = pltpu.make_async_remote_copy(
        src_ref=att_v, dst_ref=evict_ref.at[0], send_sem=evict_send, recv_sem=evict_recv, device_id=(mirror, t), device_id_type=MESH
    )
    fwd_move = pltpu.make_async_remote_copy(
        src_ref=norm_v, dst_ref=fwd_ref.at[0], send_sem=fwd_send, recv_sem=fwd_recv, device_id=(p + 1, t), device_id_type=MESH
    )

    def sum_moves(which, buffer, sends, recvs):
        return [
            pltpu.make_async_remote_copy(
                src_ref=sum_v.at[which], dst_ref=buffer.at[d - 1], send_sem=sends.at[d - 1], recv_sem=recvs.at[d - 1],
                device_id=(p, lax.rem(t + d, members)), device_id_type=MESH,
            )
            for d in range(1, members)
        ]

    slot_load.wait()
    slot = slot_ref[mirror]
    for h in range(heads):
        loads[h].wait()
        for i in range(3):
            send_v[h, i] = jnp.where(slot == 1, held_v[h, 1, i], held_v[h, 0, i])
        if h == 0:
            pl.semaphore_wait(barrier, members + one(paired) + one(has_up) + one(has_down))
        pl.when(paired)(stash[h].start)

    pl.when(has_down)(cot_move.start)

    @pl.when(to_self)
    def _():
        own = pltpu.make_async_copy(send_v, back_v, self_sem)
        own.start()
        own.wait()

    @pl.when(p == last)
    def _():
        back_v[...] = jnp.zeros_like(back_v)
        cot_v[...] = jnp.zeros_like(cot_v)

    rows = lax.broadcasted_iota(jnp.int32, (HS, HS), 0)
    causal = rows >= lax.broadcasted_iota(jnp.int32, (HS, HS), 1)
    qkv_load.wait()
    gain_load.wait()
    squares = jnp.zeros((HS, HS), F32)
    for h in range(heads):
        cols = pl.ds(h * HS, HS)
        probs = softmax_rows(qkv_v[0, :, cols], qkv_v[1, :, cols], causal)
        out = dot(probs.astype(BF16), qkv_v[2, :, cols], ((1,), (0,))).astype(BF16)
        att_v[:, cols] = out
        out = out.astype(F32)
        squares += out * out
    sum_v[0] = jnp.broadcast_to(as_row(squares), (8, HS))
    now_moves = sum_moves(0, sums_now, now_send, now_recv)
    for move in now_moves:
        move.start()
    for move in now_moves:
        move.wait_recv()
    total = sum_v[0, 0:1]
    for d in range(members - 1):
        total += sums_now[d, 0:1]
    ratio = as_columns(lax.rsqrt(total / feats + EPS))
    for h in range(heads):
        cols = pl.ds(h * HS, HS)
        norm_v[:, cols] = (att_v[:, cols].astype(F32) * ratio * gain_ref[cols][None, :]).astype(BF16)
    pl.when(has_up)(fwd_move.start)

    @pl.when(p == 0)
    def _():
        grad_v[0] = jnp.zeros_like(grad_v[0])
        zeros = pltpu.make_async_copy(grad_v.at[0], fwd_ref.at[0], zero_sem)
        zeros.start()
        zeros.wait()

    pl.when(has_up)(cot_move.wait_recv)
    squares = jnp.zeros((HS, HS), F32)
    dots = jnp.zeros((HS, HS), F32)
    for h in range(heads):
        cols = pl.ds(h * HS, HS)
        pl.when(paired)(stash[h].wait_send)
        if h == heads - 1:
            evict_move.start()
        pl.when(paired)(stash[h].wait_recv)
        probs = softmax_rows(back_v[h, 0], back_v[h, 1], causal)
        prob_v[h] = probs
        probs = probs.astype(BF16)
        pb_v[h] = probs
        out = dot(probs, back_v[h, 2], ((1,), (0,))).astype(BF16)
        ob_v[h] = out
        out = out.astype(F32)
        squares += out * out
        dots += gain_ref[cols][None, :] * cot_v[:, cols].astype(F32) * out
    sum_v[1] = jnp.concatenate([as_row(squares), as_row(dots), jnp.zeros((6, HS), F32)], axis=0)
    back_moves = sum_moves(1, sums_back, bsum_send, bsum_recv)
    for move in back_moves:
        move.start()
    for move in back_moves:
        move.wait_recv()
    total = sum_v[1]
    for d in range(members - 1):
        total += sums_back[d]
    back_ratio = lax.rsqrt(total[0:1] / feats + EPS)
    pull = as_columns(back_ratio**3 * total[1:2] / feats)
    back_ratio = as_columns(back_ratio)

    for h in range(heads):
        cols = pl.ds(h * HS, HS)
        scaled = gain_ref[cols][None, :] * cot_v[:, cols].astype(F32)
        d_out = (back_ratio * scaled - ob_v[h].astype(F32) * pull).astype(BF16)
        probs = prob_v[h]
        d_values = dot(pb_v[h], d_out, ((0,), (0,)))
        d_probs = dot(d_out, back_v[h, 2], ((1,), (1,)))
        delta = jnp.sum(probs * d_probs, axis=-1, keepdims=True)
        d_scores = (probs * (d_probs - delta) * HS ** (-0.5)).astype(BF16)
        grad_v[0, :, cols] = dot(d_scores, back_v[h, 1], ((1,), (0,))).astype(BF16)
        grad_v[1, :, cols] = dot(d_scores, back_v[h, 0], ((0,), (0,))).astype(BF16)
        grad_v[2, :, cols] = d_values.astype(BF16)
    grads_out = pltpu.make_async_copy(grad_v, grads_ref.at[0], grad_sem)
    grads_out.start()

    pl.when(has_down)(cot_move.wait_send)
    pl.when(has_up)(fwd_move.wait_send)
    pl.when(has_down)(fwd_move.wait_recv)
    for move in now_moves + back_moves:
        move.wait_send()
    grads_out.wait()
    evict_move.wait()


def hand_over(fwd_in, grads_in, evict_in, fwd_out, grads_out, evict_out, sems):
    moves = [
        pltpu.make_async_copy(fwd_in, fwd_out, sems.at[0]),
        pltpu.make_async_copy(grads_in, grads_out, sems.at[1]),
        pltpu.make_async_copy(evict_in, evict_out, sems.at[2]),
    ]
    for move in moves:
        move.start()
    for move in moves:
        move.wait()


def shards(sections, members, qkv_now, held_stash, cotangent, norm_gain, fetch_slot):
    rows, width = cotangent.shape[1:]
    heads = width // HS
    anywhere = pl.BlockSpec(memory_space=pl.ANY)
    dma = pltpu.SemaphoreType.DMA
    in_hbm = functools.partial(pltpu.with_memory_space_constraint, memory_space=pltpu.HBM)
    results = pl.pallas_call(
        functools.partial(kernel, sections, members, heads, float(width * members)),
        name="section_step",
        out_shape=(
            pltpu.VMEM((1, rows, width), BF16),
            pltpu.VMEM((1, 3, rows, width), BF16),
            pltpu.VMEM((1, rows, width), BF16),
        ),
        in_specs=[anywhere] * 5,
        out_specs=(anywhere, anywhere, anywhere),
        scratch_shapes=[
            pltpu.VMEM((heads, 2, 3, rows, HS), BF16),
            pltpu.VMEM((heads, 3, rows, HS), BF16),
            pltpu.VMEM((heads, 3, rows, HS), BF16),
            pltpu.VMEM((3, rows, width), BF16),
            pltpu.VMEM((rows, width), BF16),
            pltpu.VMEM((rows, width), BF16),
            pltpu.VMEM((rows, width), BF16),
            pltpu.VMEM((heads, rows, rows), F32),
            pltpu.VMEM((heads, rows, rows), BF16),
            pltpu.VMEM((heads, rows, HS), BF16),
            pltpu.VMEM((3, rows, width), BF16),
            pltpu.VMEM((2, 8, rows), F32),
            pltpu.VMEM((members - 1, 8, rows), F32),
            pltpu.VMEM((members - 1, 8, rows), F32),
            pltpu.VMEM((width,), F32),
            pltpu.SMEM((sections,), jnp.int32),
            dma, dma, dma((heads,)), dma, dma, dma, dma,
            dma((heads,)), dma((heads,)), dma, dma, dma, dma, dma, dma,
            dma((members - 1,)), dma((members - 1,)), dma((members - 1,)), dma((members - 1,)),
        ],
        compiler_params=pltpu.CompilerParams(collective_id=0, has_side_effects=True, vmem_limit_bytes=24 * 1024 * 1024),
    )(in_hbm(qkv_now), in_hbm(held_stash), in_hbm(cotangent), in_hbm(norm_gain), in_hbm(fetch_slot))
    return pl.pallas_call(
        hand_over,
        name="hand_over",
        out_shape=tuple(pltpu.HBM(r.shape, r.dtype) for r in results),
        in_specs=[pl.BlockSpec(memory_space=pltpu.VMEM)] * 3,
        out_specs=(anywhere,) * 3,
        scratch_shapes=[dma((3,))],
    )(*[pltpu.with_memory_space_constraint(r, memory_space=pltpu.VMEM) for r in results])


def solution(mesh):
    return jax.shard_map(
        functools.partial(shards, mesh.shape["pipe"], mesh.shape["tensor"]),
        mesh=mesh,
        in_specs=(
            P("pipe", None, None, "tensor"),
            P("pipe", None, None, None, "tensor"),
            P("pipe", None, "tensor"),
            P("tensor"),
            P(),
        ),
        out_specs=(
            P("pipe", None, "tensor"),
            P("pipe", None, None, "tensor"),
            P("pipe", None, "tensor"),
        ),
        check_vma=False,
    )
```

```python
import functools

import jax
import jax.numpy as jnp
from jax import lax
from jax.experimental import pallas as pl
from jax.experimental.pallas import tpu as pltpu
from jax.sharding import PartitionSpec as P

MESH = pl.DeviceIdType.MESH
HS = 128
EPS = 1e-05
F32 = jnp.float32
BF16 = jnp.bfloat16


def dot(x, y, dims):
    return lax.dot_general(x, y, (dims, ((), ())), preferred_element_type=F32)


def softmax_rows(queries, keys, causal):
    scores = dot(queries, keys, ((1,), (1,))) * HS ** (-0.5)
    masked = jnp.where(causal, scores, -1e30)
    expo = jnp.exp(masked - jnp.max(masked, axis=-1, keepdims=True))
    return expo / jnp.sum(expo, axis=-1, keepdims=True)


def as_row(partial):
    return jnp.sum(partial.T, axis=0, keepdims=True)


def as_columns(row):
    return jnp.broadcast_to(row, (HS, row.shape[1])).T


def kernel(
    sections, members, heads, feats,
    qkv_ref, held_ref, cot_ref, gain_hbm, slot_hbm,
    fwd_ref, grads_ref, evict_ref,
    held_v, send_v, back_v, qkv_v, cot_v, att_v, norm_v, prob_v, pb_v, ob_v, grad_v, part_v,
    sum_v, sums_now, sums_back,
    gain_ref, slot_ref, gain_sem, slot_sem, held_sem, qkv_sem, self_sem, zero_sem, grad_sem,
    stash_send, stash_recv, cot_send, cot_recv, evict_send, evict_recv, fwd_send, fwd_recv,
    now_send, now_recv, bsum_send, bsum_recv, up_ready, down_ready,
):
    p = lax.axis_index("pipe")
    t = lax.axis_index("tensor")
    last = sections - 1
    mirror = last - p
    target = last - 1 - p
    has_up = p < last
    has_down = p > 0
    to_self = target == p
    late = p >= sections // 2
    early = jnp.logical_not(late)
    core = lax.rem(p, 2)
    yh = lax.rem(p, 8) // 2
    at_once = late & (core == 1) & (yh == 1)
    behind = late & jnp.logical_not(at_once)
    paired = has_up & jnp.logical_not(to_self)

    slot_load = pltpu.make_async_copy(slot_hbm, slot_ref, slot_sem)
    slot_load.start()
    gain_load = pltpu.make_async_copy(gain_hbm, gain_ref, gain_sem)
    loads = []
    for h in range(heads):
        loads.append(pltpu.make_async_copy(held_ref.at[0, :, :, :, pl.ds(h * HS, HS)], held_v.at[h], held_sem.at[h]))
        loads[h].start()
    qkv_load = pltpu.make_async_copy(qkv_ref.at[0], qkv_v, qkv_sem)
    qkv_load.start()
    gain_load.start()

    barrier = pltpu.get_barrier_semaphore()

    def greet(section, member):
        pl.semaphore_signal(barrier, inc=1, device_id=(section, member), device_id_type=MESH)

    greet(mirror, t)
    pl.when(paired)(lambda: greet(target, t))
    for d in range(1, members):
        greet(p, lax.rem(t + d, members))

    def one(flag):
        return jnp.where(flag, 1, 0)

    stash = [
        pltpu.make_async_remote_copy(
            src_ref=send_v.at[h], dst_ref=back_v.at[h], send_sem=stash_send.at[h], recv_sem=stash_recv.at[h],
            device_id=(target, t), device_id_type=MESH,
        )
        for h in range(heads)
    ]
    cot_move = pltpu.make_async_remote_copy(
        src_ref=cot_ref.at[0], dst_ref=cot_v, send_sem=cot_send, recv_sem=cot_recv, device_id=(p - 1, t), device_id_type=MESH
    )
    evict_move = pltpu.make_async_remote_copy(
        src_ref=att_v, dst_ref=evict_ref.at[0], send_sem=evict_send, recv_sem=evict_recv, device_id=(mirror, t), device_id_type=MESH
    )
    fwd_move = pltpu.make_async_remote_copy(
        src_ref=norm_v, dst_ref=fwd_ref.at[0], send_sem=fwd_send, recv_sem=fwd_recv, device_id=(p + 1, t), device_id_type=MESH
    )

    def sum_moves(which, buffer, sends, recvs):
        return [
            pltpu.make_async_remote_copy(
                src_ref=sum_v.at[which], dst_ref=buffer.at[d - 1], send_sem=sends.at[d - 1], recv_sem=recvs.at[d - 1],
                device_id=(p, lax.rem(t + d, members)), device_id_type=MESH,
            )
            for d in range(1, members)
        ]

    def choose(h):
        loads[h].wait()
        for i in range(3):
            send_v[h, i] = jnp.where(slot == 1, held_v[h, 1, i], held_v[h, 0, i])

    slot_load.wait()
    slot = slot_ref[mirror]
    for h in range(1):
        choose(h)
    pl.semaphore_wait(barrier, members + one(paired))

    for h in range(1):
        pl.when(paired)(stash[h].start)

    def vouch(sem, section):
        pl.semaphore_signal(sem, inc=1, device_id=(section, t), device_id_type=MESH)

    pl.when(has_up)(lambda: vouch(down_ready, mirror))
    pl.when(paired)(lambda: vouch(up_ready, target))

    rows = lax.broadcasted_iota(jnp.int32, (HS, HS), 0)
    causal = rows >= lax.broadcasted_iota(jnp.int32, (HS, HS), 1)
    qkv_load.wait()
    gain_load.wait()
    squares = jnp.zeros((HS, HS), F32)
    for h in range(heads):
        cols = pl.ds(h * HS, HS)
        probs = softmax_rows(qkv_v[0, :, cols], qkv_v[1, :, cols], causal)
        out = dot(probs.astype(BF16), qkv_v[2, :, cols], ((1,), (0,))).astype(BF16)
        att_v[:, cols] = out
        out = out.astype(F32)
        squares += out * out
    sum_v[0] = jnp.broadcast_to(as_row(squares), (8, HS))
    now_moves = sum_moves(0, sums_now, now_send, now_recv)
    for move in now_moves:
        move.start()
    for h in range(1, heads):
        choose(h)
        pl.when(paired)(stash[h].start)

    pl.when(at_once)(evict_move.start)
    pl.when(has_down)(lambda: pl.semaphore_wait(down_ready, 1))
    pl.when(has_down)(cot_move.start)

    @pl.when(to_self)
    def _():
        own = pltpu.make_async_copy(send_v, back_v, self_sem)
        own.start()
        own.wait()

    @pl.when(p == last)
    def _():
        back_v[...] = jnp.zeros_like(back_v)
        cot_v[...] = jnp.zeros_like(cot_v)

    for move in now_moves:
        move.wait_recv()
    total = sum_v[0, 0:1]
    for d in range(members - 1):
        total += sums_now[d, 0:1]
    ratio = as_columns(lax.rsqrt(total / feats + EPS))
    for h in range(heads):
        cols = pl.ds(h * HS, HS)
        norm_v[:, cols] = (att_v[:, cols].astype(F32) * ratio * gain_ref[cols][None, :]).astype(BF16)
    pl.when(paired)(lambda: pl.semaphore_wait(up_ready, 1))
    pl.when(has_up)(fwd_move.start)

    @pl.when(p == 0)
    def _():
        grad_v[0] = jnp.zeros_like(grad_v[0])
        zeros = pltpu.make_async_copy(grad_v.at[0], fwd_ref.at[0], zero_sem)
        zeros.start()
        zeros.wait()

    def scaled_cot(h):
        cols = pl.ds(h * HS, HS)
        return gain_ref[cols][None, :] * cot_v[:, cols].astype(F32)

    def prepare(h):
        probs = prob_v[h]
        rest = scaled_cot(h)
        d_probs = jnp.zeros((HS, HS), F32)
        for _ in range(3):
            piece = rest.astype(BF16)
            rest = rest - piece.astype(F32)
            d_probs += dot(piece, back_v[h, 2], ((1,), (1,)))
        part_v[h, 0] = probs * (d_probs - jnp.sum(probs * d_probs, axis=-1, keepdims=True)) * HS ** (-0.5)
        d_probs = dot(ob_v[h], back_v[h, 2], ((1,), (1,)))
        part_v[h, 1] = probs * (d_probs - jnp.sum(probs * d_probs, axis=-1, keepdims=True)) * HS ** (-0.5)

    pl.when(has_up)(cot_move.wait_recv)
    squares = jnp.zeros((HS, HS), F32)
    dots = jnp.zeros((HS, HS), F32)
    for h in range(heads):
        cols = pl.ds(h * HS, HS)
        if h == heads - 1:
            for move in stash:
                pl.when(paired & behind)(move.wait_send)
        if h == heads - 1:
            pl.when(behind)(evict_move.start)
        pl.when(paired)(stash[h].wait_recv)
        probs = softmax_rows(back_v[h, 0], back_v[h, 1], causal)
        prob_v[h] = probs
        probs = probs.astype(BF16)
        pb_v[h] = probs
        out = dot(probs, back_v[h, 2], ((1,), (0,))).astype(BF16)
        ob_v[h] = out
        out = out.astype(F32)
        squares += out * out
        dots += scaled_cot(h) * out
        if h < heads - 1:
            prepare(h)
    sum_v[1] = jnp.concatenate([as_row(squares), as_row(dots), jnp.zeros((6, HS), F32)], axis=0)
    back_moves = sum_moves(1, sums_back, bsum_send, bsum_recv)
    for move in back_moves:
        move.start()
    pl.when(early)(evict_move.start)
    prepare(heads - 1)
    for move in back_moves:
        move.wait_recv()
    total = sum_v[1]
    for d in range(members - 1):
        total += sums_back[d]
    back_ratio = lax.rsqrt(total[0:1] / feats + EPS)
    pull = as_columns(back_ratio**3 * total[1:2] / feats)
    back_ratio = as_columns(back_ratio)

    grad_moves = []
    for h in range(heads):
        cols = pl.ds(h * HS, HS)
        d_out = (back_ratio * scaled_cot(h) - ob_v[h].astype(F32) * pull).astype(BF16)
        d_scores = (back_ratio * part_v[h, 0] - pull * part_v[h, 1]).astype(BF16)
        grad_v[0, :, cols] = dot(d_scores, back_v[h, 1], ((1,), (0,))).astype(BF16)
        grad_v[1, :, cols] = dot(d_scores, back_v[h, 0], ((0,), (0,))).astype(BF16)
        grad_v[2, :, cols] = dot(pb_v[h], d_out, ((0,), (0,))).astype(BF16)
        grad_moves.append(pltpu.make_async_copy(grad_v.at[:, :, cols], grads_ref.at[0, :, :, cols], grad_sem.at[h]))
        grad_moves[h].start()

    pl.when(has_down)(cot_move.wait_send)
    pl.when(has_up)(fwd_move.wait_send)
    pl.when(has_down)(fwd_move.wait_recv)
    for move in now_moves + back_moves:
        move.wait_send()
    for move in stash:
        pl.when(paired & jnp.logical_not(behind))(move.wait_send)
    for move in grad_moves:
        move.wait()
    evict_move.wait()


def hand_over(fwd_in, grads_in, evict_in, fwd_out, grads_out, evict_out, sems):
    moves = [
        pltpu.make_async_copy(fwd_in, fwd_out, sems.at[0]),
        pltpu.make_async_copy(grads_in, grads_out, sems.at[1]),
        pltpu.make_async_copy(evict_in, evict_out, sems.at[2]),
    ]
    for move in moves:
        move.start()
    for move in moves:
        move.wait()


def shards(sections, members, qkv_now, held_stash, cotangent, norm_gain, fetch_slot):
    rows, width = cotangent.shape[1:]
    heads = width // HS
    anywhere = pl.BlockSpec(memory_space=pl.ANY)
    dma = pltpu.SemaphoreType.DMA
    in_hbm = functools.partial(pltpu.with_memory_space_constraint, memory_space=pltpu.HBM)
    results = pl.pallas_call(
        functools.partial(kernel, sections, members, heads, float(width * members)),
        name="section_step",
        out_shape=(
            pltpu.VMEM((1, rows, width), BF16),
            pltpu.VMEM((1, 3, rows, width), BF16),
            pltpu.VMEM((1, rows, width), BF16),
        ),
        in_specs=[anywhere] * 5,
        out_specs=(anywhere, anywhere, anywhere),
        scratch_shapes=[
            pltpu.VMEM((heads, 2, 3, rows, HS), BF16),
            pltpu.VMEM((heads, 3, rows, HS), BF16),
            pltpu.VMEM((heads, 3, rows, HS), BF16),
            pltpu.VMEM((3, rows, width), BF16),
            pltpu.VMEM((rows, width), BF16),
            pltpu.VMEM((rows, width), BF16),
            pltpu.VMEM((rows, width), BF16),
            pltpu.VMEM((heads, rows, rows), F32),
            pltpu.VMEM((heads, rows, rows), BF16),
            pltpu.VMEM((heads, rows, HS), BF16),
            pltpu.VMEM((3, rows, width), BF16),
            pltpu.VMEM((heads, 2, rows, rows), F32),
            pltpu.VMEM((2, 8, rows), F32),
            pltpu.VMEM((members - 1, 8, rows), F32),
            pltpu.VMEM((members - 1, 8, rows), F32),
            pltpu.VMEM((width,), F32),
            pltpu.SMEM((sections,), jnp.int32),
            dma, dma, dma((heads,)), dma, dma, dma, dma((heads,)),
            dma((heads,)), dma((heads,)), dma, dma, dma, dma, dma, dma,
            dma((members - 1,)), dma((members - 1,)), dma((members - 1,)), dma((members - 1,)),
            pltpu.SemaphoreType.REGULAR, pltpu.SemaphoreType.REGULAR,
        ],
        compiler_params=pltpu.CompilerParams(collective_id=0, has_side_effects=True, vmem_limit_bytes=24 * 1024 * 1024),
    )(in_hbm(qkv_now), in_hbm(held_stash), in_hbm(cotangent), in_hbm(norm_gain), in_hbm(fetch_slot))
    return pl.pallas_call(
        hand_over,
        name="hand_over",
        out_shape=tuple(pltpu.HBM(r.shape, r.dtype) for r in results),
        in_specs=[pl.BlockSpec(memory_space=pltpu.VMEM)] * 3,
        out_specs=(anywhere,) * 3,
        scratch_shapes=[dma((3,))],
    )(*[pltpu.with_memory_space_constraint(r, memory_space=pltpu.VMEM) for r in results])


def solution(mesh):
    return jax.shard_map(
        functools.partial(shards, mesh.shape["pipe"], mesh.shape["tensor"]),
        mesh=mesh,
        in_specs=(
            P("pipe", None, None, "tensor"),
            P("pipe", None, None, None, "tensor"),
            P("pipe", None, "tensor"),
            P("tensor"),
            P(),
        ),
        out_specs=(
            P("pipe", None, "tensor"),
            P("pipe", None, None, "tensor"),
            P("pipe", None, "tensor"),
        ),
        check_vma=False,
    )
```

```python
import functools

import jax
import jax.numpy as jnp
from jax import lax
from jax.experimental import pallas as pl
from jax.experimental.pallas import tpu as pltpu
from jax.sharding import PartitionSpec as P

MESH = pl.DeviceIdType.MESH
HS = 128
EPS = 1e-05
F32 = jnp.float32
BF16 = jnp.bfloat16


def dot(x, y, dims):
    return lax.dot_general(x, y, (dims, ((), ())), preferred_element_type=F32)


def softmax_rows(queries, keys, causal):
    scores = dot(queries, keys, ((1,), (1,))) * HS ** (-0.5)
    masked = jnp.where(causal, scores, -1e30)
    expo = jnp.exp(masked - jnp.max(masked, axis=-1, keepdims=True))
    return expo / jnp.sum(expo, axis=-1, keepdims=True)


def as_row(partial):
    return jnp.sum(partial.T, axis=0, keepdims=True)


def as_columns(row):
    return jnp.broadcast_to(row, (HS, row.shape[1])).T


def kernel(
    sections, members, heads, feats,
    qkv_ref, held_ref, cot_ref, gain_hbm, slot_hbm,
    fwd_ref, grads_ref, evict_ref,
    held_v, send_v, back_v, qkv_v, cot_v, att_v, norm_v, prob_v, pb_v, ob_v, grad_v, part_v,
    sum_v, sums_now, sums_back,
    gain_ref, slot_ref, gain_sem, slot_sem, held_sem, qkv_sem, self_sem, zero_sem, grad_sem,
    stash_send, stash_recv, cot_send, cot_recv, evict_send, evict_recv, fwd_send, fwd_recv,
    now_send, now_recv, bsum_send, bsum_recv, up_ready, down_ready,
):
    p = lax.axis_index("pipe")
    t = lax.axis_index("tensor")
    last = sections - 1
    mirror = last - p
    target = last - 1 - p
    has_up = p < last
    has_down = p > 0
    to_self = target == p
    late = p >= sections // 2
    early = jnp.logical_not(late)
    core = lax.rem(p, 2)
    yh = lax.rem(p, 8) // 2
    at_once = late & (core == 1) & (yh == 1)
    behind = late & jnp.logical_not(at_once)
    paired = has_up & jnp.logical_not(to_self)

    slot_load = pltpu.make_async_copy(slot_hbm, slot_ref, slot_sem)
    slot_load.start()
    gain_load = pltpu.make_async_copy(gain_hbm, gain_ref, gain_sem)
    loads = []
    for h in range(heads):
        loads.append(pltpu.make_async_copy(held_ref.at[0, :, :, :, pl.ds(h * HS, HS)], held_v.at[h], held_sem.at[h]))
        loads[h].start()
    qkv_load = pltpu.make_async_copy(qkv_ref.at[0], qkv_v, qkv_sem)
    qkv_load.start()
    gain_load.start()

    barrier = pltpu.get_barrier_semaphore()

    def greet(section, member):
        pl.semaphore_signal(barrier, inc=1, device_id=(section, member), device_id_type=MESH)

    greet(mirror, t)
    pl.when(paired)(lambda: greet(target, t))
    for d in range(1, members):
        greet(p, lax.rem(t + d, members))

    def one(flag):
        return jnp.where(flag, 1, 0)

    stash = [
        pltpu.make_async_remote_copy(
            src_ref=send_v.at[h], dst_ref=back_v.at[h], send_sem=stash_send.at[h], recv_sem=stash_recv.at[h],
            device_id=(target, t), device_id_type=MESH,
        )
        for h in range(heads)
    ]
    cot_move = pltpu.make_async_remote_copy(
        src_ref=cot_ref.at[0], dst_ref=cot_v, send_sem=cot_send, recv_sem=cot_recv, device_id=(p - 1, t), device_id_type=MESH
    )
    evict_move = pltpu.make_async_remote_copy(
        src_ref=att_v, dst_ref=evict_ref.at[0], send_sem=evict_send, recv_sem=evict_recv, device_id=(mirror, t), device_id_type=MESH
    )
    fwd_move = pltpu.make_async_remote_copy(
        src_ref=norm_v, dst_ref=fwd_ref.at[0], send_sem=fwd_send, recv_sem=fwd_recv, device_id=(p + 1, t), device_id_type=MESH
    )

    def sum_moves(which, buffer, sends, recvs):
        return [
            pltpu.make_async_remote_copy(
                src_ref=sum_v.at[which], dst_ref=buffer.at[d - 1], send_sem=sends.at[d - 1], recv_sem=recvs.at[d - 1],
                device_id=(p, lax.rem(t + d, members)), device_id_type=MESH,
            )
            for d in range(1, members)
        ]

    def choose(h):
        loads[h].wait()
        for i in range(3):
            send_v[h, i] = jnp.where(slot == 1, held_v[h, 1, i], held_v[h, 0, i])

    slot_load.wait()
    slot = slot_ref[mirror]
    for h in range(1):
        choose(h)
    pl.semaphore_wait(barrier, members + one(paired))

    for h in range(1):
        pl.when(paired)(stash[h].start)

    def vouch(sem, section):
        pl.semaphore_signal(sem, inc=1, device_id=(section, t), device_id_type=MESH)

    pl.when(has_up)(lambda: vouch(down_ready, mirror))
    pl.when(paired)(lambda: vouch(up_ready, target))

    rows = lax.broadcasted_iota(jnp.int32, (HS, HS), 0)
    causal = rows >= lax.broadcasted_iota(jnp.int32, (HS, HS), 1)
    qkv_load.wait()
    gain_load.wait()
    squares = jnp.zeros((HS, HS), F32)
    for h in range(heads):
        cols = pl.ds(h * HS, HS)
        probs = softmax_rows(qkv_v[0, :, cols], qkv_v[1, :, cols], causal)
        out = dot(probs.astype(BF16), qkv_v[2, :, cols], ((1,), (0,))).astype(BF16)
        att_v[:, cols] = out
        out = out.astype(F32)
        squares += out * out
    sum_v[0] = jnp.broadcast_to(as_row(squares), (8, HS))
    now_moves = sum_moves(0, sums_now, now_send, now_recv)
    for move in now_moves:
        move.start()
    for h in range(1, heads):
        if h == 4:
            pl.when(has_down)(lambda: pl.semaphore_wait(down_ready, 1))
            pl.when(has_down)(cot_move.start)
        choose(h)
        pl.when(paired)(stash[h].start)

    pl.when(at_once)(evict_move.start)

    @pl.when(to_self)
    def _():
        own = pltpu.make_async_copy(send_v, back_v, self_sem)
        own.start()
        own.wait()

    @pl.when(p == last)
    def _():
        back_v[...] = jnp.zeros_like(back_v)
        cot_v[...] = jnp.zeros_like(cot_v)

    for move in now_moves:
        move.wait_recv()
    total = sum_v[0, 0:1]
    for d in range(members - 1):
        total += sums_now[d, 0:1]
    ratio = as_columns(lax.rsqrt(total / feats + EPS))
    for h in range(heads):
        cols = pl.ds(h * HS, HS)
        norm_v[:, cols] = (att_v[:, cols].astype(F32) * ratio * gain_ref[cols][None, :]).astype(BF16)
    pl.when(paired)(lambda: pl.semaphore_wait(up_ready, 1))
    pl.when(has_up)(fwd_move.start)

    @pl.when(p == 0)
    def _():
        grad_v[0] = jnp.zeros_like(grad_v[0])
        zeros = pltpu.make_async_copy(grad_v.at[0], fwd_ref.at[0], zero_sem)
        zeros.start()
        zeros.wait()

    def scaled_cot(h):
        cols = pl.ds(h * HS, HS)
        return gain_ref[cols][None, :] * cot_v[:, cols].astype(F32)

    def prepare(h):
        probs = prob_v[h]
        rest = scaled_cot(h)
        d_probs = jnp.zeros((HS, HS), F32)
        for _ in range(3):
            piece = rest.astype(BF16)
            rest = rest - piece.astype(F32)
            d_probs += dot(piece, back_v[h, 2], ((1,), (1,)))
        part_v[h, 0] = probs * (d_probs - jnp.sum(probs * d_probs, axis=-1, keepdims=True)) * HS ** (-0.5)
        d_probs = dot(ob_v[h], back_v[h, 2], ((1,), (1,)))
        part_v[h, 1] = probs * (d_probs - jnp.sum(probs * d_probs, axis=-1, keepdims=True)) * HS ** (-0.5)

    pl.when(has_up)(cot_move.wait_recv)
    squares = jnp.zeros((HS, HS), F32)
    dots = jnp.zeros((HS, HS), F32)
    for h in range(heads):
        cols = pl.ds(h * HS, HS)
        if h == heads - 1:
            for move in stash:
                pl.when(paired & behind)(move.wait_send)
        if h == heads - 1:
            pl.when(behind)(evict_move.start)
        pl.when(paired)(stash[h].wait_recv)
        probs = softmax_rows(back_v[h, 0], back_v[h, 1], causal)
        prob_v[h] = probs
        probs = probs.astype(BF16)
        pb_v[h] = probs
        out = dot(probs, back_v[h, 2], ((1,), (0,))).astype(BF16)
        ob_v[h] = out
        out = out.astype(F32)
        squares += out * out
        dots += scaled_cot(h) * out
        if h < heads - 1:
            prepare(h)
    sum_v[1] = jnp.concatenate([as_row(squares), as_row(dots), jnp.zeros((6, HS), F32)], axis=0)
    back_moves = sum_moves(1, sums_back, bsum_send, bsum_recv)
    for move in back_moves:
        move.start()
    pl.when(jnp.logical_not(at_once | behind))(evict_move.start)
    prepare(heads - 1)
    for move in back_moves:
        move.wait_recv()
    total = sum_v[1]
    for d in range(members - 1):
        total += sums_back[d]
    back_ratio = lax.rsqrt(total[0:1] / feats + EPS)
    pull = as_columns(back_ratio**3 * total[1:2] / feats)
    back_ratio = as_columns(back_ratio)

    grad_moves = []
    for h in range(heads):
        cols = pl.ds(h * HS, HS)
        d_out = (back_ratio * scaled_cot(h) - ob_v[h].astype(F32) * pull).astype(BF16)
        d_scores = (back_ratio * part_v[h, 0] - pull * part_v[h, 1]).astype(BF16)
        grad_v[0, :, cols] = dot(d_scores, back_v[h, 1], ((1,), (0,))).astype(BF16)
        grad_v[1, :, cols] = dot(d_scores, back_v[h, 0], ((0,), (0,))).astype(BF16)
        grad_v[2, :, cols] = dot(pb_v[h], d_out, ((0,), (0,))).astype(BF16)
        grad_moves.append(pltpu.make_async_copy(grad_v.at[:, :, cols], grads_ref.at[0, :, :, cols], grad_sem.at[h]))
        grad_moves[h].start()

    pl.when(has_down)(cot_move.wait_send)
    pl.when(has_up)(fwd_move.wait_send)
    pl.when(has_down)(fwd_move.wait_recv)
    for move in now_moves + back_moves:
        move.wait_send()
    for move in stash:
        pl.when(paired & jnp.logical_not(behind))(move.wait_send)
    for move in grad_moves:
        move.wait()
    evict_move.wait()


def hand_over(fwd_in, grads_in, evict_in, fwd_out, grads_out, evict_out, sems):
    moves = [
        pltpu.make_async_copy(fwd_in, fwd_out, sems.at[0]),
        pltpu.make_async_copy(grads_in, grads_out, sems.at[1]),
        pltpu.make_async_copy(evict_in, evict_out, sems.at[2]),
    ]
    for move in moves:
        move.start()
    for move in moves:
        move.wait()


def shards(sections, members, qkv_now, held_stash, cotangent, norm_gain, fetch_slot):
    rows, width = cotangent.shape[1:]
    heads = width // HS
    anywhere = pl.BlockSpec(memory_space=pl.ANY)
    dma = pltpu.SemaphoreType.DMA
    in_hbm = functools.partial(pltpu.with_memory_space_constraint, memory_space=pltpu.HBM)
    results = pl.pallas_call(
        functools.partial(kernel, sections, members, heads, float(width * members)),
        name="section_step",
        out_shape=(
            pltpu.VMEM((1, rows, width), BF16),
            pltpu.VMEM((1, 3, rows, width), BF16),
            pltpu.VMEM((1, rows, width), BF16),
        ),
        in_specs=[anywhere] * 5,
        out_specs=(anywhere, anywhere, anywhere),
        scratch_shapes=[
            pltpu.VMEM((heads, 2, 3, rows, HS), BF16),
            pltpu.VMEM((heads, 3, rows, HS), BF16),
            pltpu.VMEM((heads, 3, rows, HS), BF16),
            pltpu.VMEM((3, rows, width), BF16),
            pltpu.VMEM((rows, width), BF16),
            pltpu.VMEM((rows, width), BF16),
            pltpu.VMEM((rows, width), BF16),
            pltpu.VMEM((heads, rows, rows), F32),
            pltpu.VMEM((heads, rows, rows), BF16),
            pltpu.VMEM((heads, rows, HS), BF16),
            pltpu.VMEM((3, rows, width), BF16),
            pltpu.VMEM((heads, 2, rows, rows), F32),
            pltpu.VMEM((2, 8, rows), F32),
            pltpu.VMEM((members - 1, 8, rows), F32),
            pltpu.VMEM((members - 1, 8, rows), F32),
            pltpu.VMEM((width,), F32),
            pltpu.SMEM((sections,), jnp.int32),
            dma, dma, dma((heads,)), dma, dma, dma, dma((heads,)),
            dma((heads,)), dma((heads,)), dma, dma, dma, dma, dma, dma,
            dma((members - 1,)), dma((members - 1,)), dma((members - 1,)), dma((members - 1,)),
            pltpu.SemaphoreType.REGULAR, pltpu.SemaphoreType.REGULAR,
        ],
        compiler_params=pltpu.CompilerParams(collective_id=0, has_side_effects=True, vmem_limit_bytes=24 * 1024 * 1024),
    )(in_hbm(qkv_now), in_hbm(held_stash), in_hbm(cotangent), in_hbm(norm_gain), in_hbm(fetch_slot))
    return pl.pallas_call(
        hand_over,
        name="hand_over",
        out_shape=tuple(pltpu.HBM(r.shape, r.dtype) for r in results),
        in_specs=[pl.BlockSpec(memory_space=pltpu.VMEM)] * 3,
        out_specs=(anywhere,) * 3,
        scratch_shapes=[dma((3,))],
    )(*[pltpu.with_memory_space_constraint(r, memory_space=pltpu.VMEM) for r in results])


def solution(mesh):
    return jax.shard_map(
        functools.partial(shards, mesh.shape["pipe"], mesh.shape["tensor"]),
        mesh=mesh,
        in_specs=(
            P("pipe", None, None, "tensor"),
            P("pipe", None, None, None, "tensor"),
            P("pipe", None, "tensor"),
            P("tensor"),
            P(),
        ),
        out_specs=(
            P("pipe", None, "tensor"),
            P("pipe", None, None, "tensor"),
            P("pipe", None, "tensor"),
        ),
        check_vma=False,
    )
```

```python
import functools

import jax
import jax.numpy as jnp
from jax import lax
from jax.experimental import pallas as pl
from jax.experimental.pallas import tpu as pltpu
from jax.sharding import PartitionSpec as P

MESH = pl.DeviceIdType.MESH
HS = 128
EPS = 1e-05
F32 = jnp.float32
BF16 = jnp.bfloat16


def dot(x, y, dims):
    return lax.dot_general(x, y, (dims, ((), ())), preferred_element_type=F32)


def softmax_rows(queries, keys, causal):
    scores = dot(queries, keys, ((1,), (1,))) * HS ** (-0.5)
    masked = jnp.where(causal, scores, -1e30)
    expo = jnp.exp(masked - jnp.max(masked, axis=-1, keepdims=True))
    return expo / jnp.sum(expo, axis=-1, keepdims=True)


def as_row(partial):
    return jnp.sum(partial.T, axis=0, keepdims=True)


def as_columns(row):
    return jnp.broadcast_to(row, (HS, row.shape[1])).T


def kernel(
    sections, members, heads, feats,
    qkv_ref, held_ref, cot_ref, gain_hbm, slot_hbm,
    fwd_ref, grads_ref, evict_ref,
    held_v, send_v, back_v, qkv_v, cot_v, att_v, norm_v, prob_v, pb_v, ob_v, grad_v, part_v,
    sum_v, sums_now, sums_back,
    gain_ref, slot_ref, gain_sem, slot_sem, held_sem, qkv_sem, self_sem, zero_sem, grad_sem,
    stash_send, stash_recv, cot_send, cot_recv, evict_send, evict_recv, fwd_send, fwd_recv,
    now_send, now_recv, bsum_send, bsum_recv, up_ready, down_ready,
):
    p = lax.axis_index("pipe")
    t = lax.axis_index("tensor")
    last = sections - 1
    mirror = last - p
    target = last - 1 - p
    has_up = p < last
    has_down = p > 0
    to_self = target == p
    late = p >= sections // 2
    early = jnp.logical_not(late)
    core = lax.rem(p, 2)
    yh = lax.rem(p, 8) // 2
    at_once = late & (((core == 1) & (yh == 1)) | ((core == 0) & (yh == 3) & (p // 8 == 5)))
    behind = late & jnp.logical_not(at_once)
    paired = has_up & jnp.logical_not(to_self)

    slot_load = pltpu.make_async_copy(slot_hbm, slot_ref, slot_sem)
    slot_load.start()
    gain_load = pltpu.make_async_copy(gain_hbm, gain_ref, gain_sem)
    loads = []
    for h in range(heads):
        loads.append(pltpu.make_async_copy(held_ref.at[0, :, :, :, pl.ds(h * HS, HS)], held_v.at[h], held_sem.at[h]))
        loads[h].start()
    qkv_load = pltpu.make_async_copy(qkv_ref.at[0], qkv_v, qkv_sem)
    qkv_load.start()
    gain_load.start()

    barrier = pltpu.get_barrier_semaphore()

    def greet(section, member):
        pl.semaphore_signal(barrier, inc=1, device_id=(section, member), device_id_type=MESH)

    greet(mirror, t)
    pl.when(paired)(lambda: greet(target, t))
    for d in range(1, members):
        greet(p, lax.rem(t + d, members))

    def one(flag):
        return jnp.where(flag, 1, 0)

    stash = [
        pltpu.make_async_remote_copy(
            src_ref=send_v.at[h], dst_ref=back_v.at[h], send_sem=stash_send.at[h], recv_sem=stash_recv.at[h],
            device_id=(target, t), device_id_type=MESH,
        )
        for h in range(heads)
    ]
    cot_move = pltpu.make_async_remote_copy(
        src_ref=cot_ref.at[0], dst_ref=cot_v, send_sem=cot_send, recv_sem=cot_recv, device_id=(p - 1, t), device_id_type=MESH
    )
    evict_move = pltpu.make_async_remote_copy(
        src_ref=att_v, dst_ref=evict_ref.at[0], send_sem=evict_send, recv_sem=evict_recv, device_id=(mirror, t), device_id_type=MESH
    )
    fwd_move = pltpu.make_async_remote_copy(
        src_ref=norm_v, dst_ref=fwd_ref.at[0], send_sem=fwd_send, recv_sem=fwd_recv, device_id=(p + 1, t), device_id_type=MESH
    )

    def sum_moves(which, buffer, sends, recvs):
        return [
            pltpu.make_async_remote_copy(
                src_ref=sum_v.at[which], dst_ref=buffer.at[d - 1], send_sem=sends.at[d - 1], recv_sem=recvs.at[d - 1],
                device_id=(p, lax.rem(t + d, members)), device_id_type=MESH,
            )
            for d in range(1, members)
        ]

    def choose(h):
        loads[h].wait()
        for i in range(3):
            send_v[h, i] = jnp.where(slot == 1, held_v[h, 1, i], held_v[h, 0, i])

    slot_load.wait()
    slot = slot_ref[mirror]
    for h in range(1):
        choose(h)
    def enter():
        pl.semaphore_wait(barrier, members + one(paired))
        for h in range(1):
            pl.when(paired)(stash[h].start)
        pl.when(has_up)(lambda: vouch(down_ready, mirror))
        pl.when(paired)(lambda: vouch(up_ready, target))

    def vouch(sem, section):
        pl.semaphore_signal(sem, inc=1, device_id=(section, t), device_id_type=MESH)

    pl.when(late)(enter)

    rows = lax.broadcasted_iota(jnp.int32, (HS, HS), 0)
    causal = rows >= lax.broadcasted_iota(jnp.int32, (HS, HS), 1)
    qkv_load.wait()
    gain_load.wait()
    squares = jnp.zeros((HS, HS), F32)
    for h in range(heads):
        cols = pl.ds(h * HS, HS)
        probs = softmax_rows(qkv_v[0, :, cols], qkv_v[1, :, cols], causal)
        out = dot(probs.astype(BF16), qkv_v[2, :, cols], ((1,), (0,))).astype(BF16)
        att_v[:, cols] = out
        out = out.astype(F32)
        squares += out * out
    sum_v[0] = jnp.broadcast_to(as_row(squares), (8, HS))
    pl.when(early)(enter)
    now_moves = sum_moves(0, sums_now, now_send, now_recv)
    for move in now_moves:
        move.start()
    for h in range(1, heads):
        if h == 3:
            pl.when(has_down)(lambda: pl.semaphore_wait(down_ready, 1))
            pl.when(has_down)(cot_move.start)
        choose(h)
        pl.when(paired)(stash[h].start)

    pl.when(at_once)(evict_move.start)

    @pl.when(to_self)
    def _():
        own = pltpu.make_async_copy(send_v, back_v, self_sem)
        own.start()
        own.wait()

    @pl.when(p == last)
    def _():
        back_v[...] = jnp.zeros_like(back_v)
        cot_v[...] = jnp.zeros_like(cot_v)

    for move in now_moves:
        move.wait_recv()
    total = sum_v[0, 0:1]
    for d in range(members - 1):
        total += sums_now[d, 0:1]
    ratio = as_columns(lax.rsqrt(total / feats + EPS))
    for h in range(heads):
        cols = pl.ds(h * HS, HS)
        norm_v[:, cols] = (att_v[:, cols].astype(F32) * ratio * gain_ref[cols][None, :]).astype(BF16)
    pl.when(paired)(lambda: pl.semaphore_wait(up_ready, 1))
    pl.when(has_up)(fwd_move.start)

    @pl.when(p == 0)
    def _():
        grad_v[0] = jnp.zeros_like(grad_v[0])
        zeros = pltpu.make_async_copy(grad_v.at[0], fwd_ref.at[0], zero_sem)
        zeros.start()
        zeros.wait()

    def scaled_cot(h):
        cols = pl.ds(h * HS, HS)
        return gain_ref[cols][None, :] * cot_v[:, cols].astype(F32)

    def prepare(h):
        probs = prob_v[h]
        rest = scaled_cot(h)
        d_probs = jnp.zeros((HS, HS), F32)
        for _ in range(3):
            piece = rest.astype(BF16)
            rest = rest - piece.astype(F32)
            d_probs += dot(piece, back_v[h, 2], ((1,), (1,)))
        part_v[h, 0] = probs * (d_probs - jnp.sum(probs * d_probs, axis=-1, keepdims=True)) * HS ** (-0.5)
        d_probs = dot(ob_v[h], back_v[h, 2], ((1,), (1,)))
        part_v[h, 1] = probs * (d_probs - jnp.sum(probs * d_probs, axis=-1, keepdims=True)) * HS ** (-0.5)

    pl.when(has_up)(cot_move.wait_recv)
    squares = jnp.zeros((HS, HS), F32)
    dots = jnp.zeros((HS, HS), F32)
    for h in range(heads):
        cols = pl.ds(h * HS, HS)
        if h == heads - 1:
            for move in stash:
                pl.when(paired & behind)(move.wait_send)
        if h == heads - 1:
            pl.when(behind)(evict_move.start)
        pl.when(paired)(stash[h].wait_recv)
        probs = softmax_rows(back_v[h, 0], back_v[h, 1], causal)
        prob_v[h] = probs
        probs = probs.astype(BF16)
        pb_v[h] = probs
        out = dot(probs, back_v[h, 2], ((1,), (0,))).astype(BF16)
        ob_v[h] = out
        out = out.astype(F32)
        squares += out * out
        dots += scaled_cot(h) * out
        if h < heads - 1:
            prepare(h)
    sum_v[1] = jnp.concatenate([as_row(squares), as_row(dots), jnp.zeros((6, HS), F32)], axis=0)
    back_moves = sum_moves(1, sums_back, bsum_send, bsum_recv)
    for move in back_moves:
        move.start()
    pl.when(jnp.logical_not(at_once | behind))(evict_move.start)
    prepare(heads - 1)
    for move in back_moves:
        move.wait_recv()
    total = sum_v[1]
    for d in range(members - 1):
        total += sums_back[d]
    back_ratio = lax.rsqrt(total[0:1] / feats + EPS)
    pull = as_columns(back_ratio**3 * total[1:2] / feats)
    back_ratio = as_columns(back_ratio)

    grad_moves = []
    for h in range(heads):
        cols = pl.ds(h * HS, HS)
        d_out = (back_ratio * scaled_cot(h) - ob_v[h].astype(F32) * pull).astype(BF16)
        d_scores = (back_ratio * part_v[h, 0] - pull * part_v[h, 1]).astype(BF16)
        grad_v[0, :, cols] = dot(d_scores, back_v[h, 1], ((1,), (0,))).astype(BF16)
        grad_v[1, :, cols] = dot(d_scores, back_v[h, 0], ((0,), (0,))).astype(BF16)
        grad_v[2, :, cols] = dot(pb_v[h], d_out, ((0,), (0,))).astype(BF16)
        grad_moves.append(pltpu.make_async_copy(grad_v.at[:, :, cols], grads_ref.at[0, :, :, cols], grad_sem.at[h]))
        grad_moves[h].start()

    pl.when(has_down)(cot_move.wait_send)
    pl.when(has_up)(fwd_move.wait_send)
    pl.when(has_down)(fwd_move.wait_recv)
    for move in now_moves + back_moves:
        move.wait_send()
    for move in stash:
        pl.when(paired & jnp.logical_not(behind))(move.wait_send)
    for move in grad_moves:
        move.wait()
    evict_move.wait()


def hand_over(fwd_in, grads_in, evict_in, fwd_out, grads_out, evict_out, sems):
    moves = [
        pltpu.make_async_copy(fwd_in, fwd_out, sems.at[0]),
        pltpu.make_async_copy(grads_in, grads_out, sems.at[1]),
        pltpu.make_async_copy(evict_in, evict_out, sems.at[2]),
    ]
    for move in moves:
        move.start()
    for move in moves:
        move.wait()


def shards(sections, members, qkv_now, held_stash, cotangent, norm_gain, fetch_slot):
    rows, width = cotangent.shape[1:]
    heads = width // HS
    anywhere = pl.BlockSpec(memory_space=pl.ANY)
    dma = pltpu.SemaphoreType.DMA
    in_hbm = functools.partial(pltpu.with_memory_space_constraint, memory_space=pltpu.HBM)
    results = pl.pallas_call(
        functools.partial(kernel, sections, members, heads, float(width * members)),
        name="section_step",
        out_shape=(
            pltpu.VMEM((1, rows, width), BF16),
            pltpu.VMEM((1, 3, rows, width), BF16),
            pltpu.VMEM((1, rows, width), BF16),
        ),
        in_specs=[anywhere] * 5,
        out_specs=(anywhere, anywhere, anywhere),
        scratch_shapes=[
            pltpu.VMEM((heads, 2, 3, rows, HS), BF16),
            pltpu.VMEM((heads, 3, rows, HS), BF16),
            pltpu.VMEM((heads, 3, rows, HS), BF16),
            pltpu.VMEM((3, rows, width), BF16),
            pltpu.VMEM((rows, width), BF16),
            pltpu.VMEM((rows, width), BF16),
            pltpu.VMEM((rows, width), BF16),
            pltpu.VMEM((heads, rows, rows), F32),
            pltpu.VMEM((heads, rows, rows), BF16),
            pltpu.VMEM((heads, rows, HS), BF16),
            pltpu.VMEM((3, rows, width), BF16),
            pltpu.VMEM((heads, 2, rows, rows), F32),
            pltpu.VMEM((2, 8, rows), F32),
            pltpu.VMEM((members - 1, 8, rows), F32),
            pltpu.VMEM((members - 1, 8, rows), F32),
            pltpu.VMEM((width,), F32),
            pltpu.SMEM((sections,), jnp.int32),
            dma, dma, dma((heads,)), dma, dma, dma, dma((heads,)),
            dma((heads,)), dma((heads,)), dma, dma, dma, dma, dma, dma,
            dma((members - 1,)), dma((members - 1,)), dma((members - 1,)), dma((members - 1,)),
            pltpu.SemaphoreType.REGULAR, pltpu.SemaphoreType.REGULAR,
        ],
        compiler_params=pltpu.CompilerParams(collective_id=0, has_side_effects=True, vmem_limit_bytes=24 * 1024 * 1024),
    )(in_hbm(qkv_now), in_hbm(held_stash), in_hbm(cotangent), in_hbm(norm_gain), in_hbm(fetch_slot))
    return pl.pallas_call(
        hand_over,
        name="hand_over",
        out_shape=tuple(pltpu.HBM(r.shape, r.dtype) for r in results),
        in_specs=[pl.BlockSpec(memory_space=pltpu.VMEM)] * 3,
        out_specs=(anywhere,) * 3,
        scratch_shapes=[dma((3,))],
    )(*[pltpu.with_memory_space_constraint(r, memory_space=pltpu.VMEM) for r in results])


def solution(mesh):
    return jax.shard_map(
        functools.partial(shards, mesh.shape["pipe"], mesh.shape["tensor"]),
        mesh=mesh,
        in_specs=(
            P("pipe", None, None, "tensor"),
            P("pipe", None, None, None, "tensor"),
            P("pipe", None, "tensor"),
            P("tensor"),
            P(),
        ),
        out_specs=(
            P("pipe", None, "tensor"),
            P("pipe", None, None, "tensor"),
            P("pipe", None, "tensor"),
        ),
        check_vma=False,
    )
```

```python
import functools

import jax
import jax.numpy as jnp
from jax import lax
from jax.experimental import pallas as pl
from jax.experimental.pallas import tpu as pltpu
from jax.sharding import PartitionSpec as P

MESH = pl.DeviceIdType.MESH
HS = 128
EPS = 1e-05
F32 = jnp.float32
BF16 = jnp.bfloat16


def dot(x, y, dims):
    return lax.dot_general(x, y, (dims, ((), ())), preferred_element_type=F32)


def softmax_rows(queries, keys, causal):
    scores = dot(queries, keys, ((1,), (1,))) * HS ** (-0.5)
    masked = jnp.where(causal, scores, -1e30)
    expo = jnp.exp(masked - jnp.max(masked, axis=-1, keepdims=True))
    return expo / jnp.sum(expo, axis=-1, keepdims=True)


def as_row(partial):
    return jnp.sum(partial.T, axis=0, keepdims=True)


def as_columns(row):
    return jnp.broadcast_to(row, (HS, row.shape[1])).T


def kernel(
    sections, members, heads, feats,
    qkv_ref, held_ref, cot_ref, gain_hbm, slot_hbm,
    fwd_ref, grads_ref, evict_ref,
    held_v, send_v, back_v, qkv_v, cot_v, att_v, norm_v, prob_v, pb_v, ob_v, grad_v, part_v,
    sum_v, sums_now, sums_back,
    gain_ref, slot_ref, gain_sem, slot_sem, held_sem, qkv_sem, self_sem, zero_sem, grad_sem,
    stash_send, stash_recv, cot_send, cot_recv, evict_send, evict_recv, fwd_send, fwd_recv,
    now_send, now_recv, bsum_send, bsum_recv, up_ready, down_ready,
):
    p = lax.axis_index("pipe")
    t = lax.axis_index("tensor")
    last = sections - 1
    mirror = last - p
    target = last - 1 - p
    has_up = p < last
    has_down = p > 0
    to_self = target == p
    late = p >= sections // 2
    early = jnp.logical_not(late)
    core = lax.rem(p, 2)
    yh = lax.rem(p, 8) // 2
    at_once = late & (((core == 1) & (yh == 1)) | ((core == 0) & (yh == 3) & (p // 8 == 5)) | ((core == 0) & (yh == 2) & (p // 8 == 6)))
    behind = late & jnp.logical_not(at_once) & jnp.logical_not((core == 1) & (yh == 2))
    paired = has_up & jnp.logical_not(to_self)

    slot_load = pltpu.make_async_copy(slot_hbm, slot_ref, slot_sem)
    slot_load.start()
    gain_load = pltpu.make_async_copy(gain_hbm, gain_ref, gain_sem)
    loads = []
    for h in range(heads):
        loads.append(pltpu.make_async_copy(held_ref.at[0, :, :, :, pl.ds(h * HS, HS)], held_v.at[h], held_sem.at[h]))
        loads[h].start()
    qkv_load = pltpu.make_async_copy(qkv_ref.at[0], qkv_v, qkv_sem)
    qkv_load.start()
    gain_load.start()

    barrier = pltpu.get_barrier_semaphore()

    def greet(section, member):
        pl.semaphore_signal(barrier, inc=1, device_id=(section, member), device_id_type=MESH)

    greet(mirror, t)
    pl.when(paired)(lambda: greet(target, t))
    for d in range(1, members):
        greet(p, lax.rem(t + d, members))

    def one(flag):
        return jnp.where(flag, 1, 0)

    stash = [
        pltpu.make_async_remote_copy(
            src_ref=send_v.at[h], dst_ref=back_v.at[h], send_sem=stash_send.at[h], recv_sem=stash_recv.at[h],
            device_id=(target, t), device_id_type=MESH,
        )
        for h in range(heads)
    ]
    cot_move = pltpu.make_async_remote_copy(
        src_ref=cot_ref.at[0], dst_ref=cot_v, send_sem=cot_send, recv_sem=cot_recv, device_id=(p - 1, t), device_id_type=MESH
    )
    evict_move = pltpu.make_async_remote_copy(
        src_ref=att_v, dst_ref=evict_ref.at[0], send_sem=evict_send, recv_sem=evict_recv, device_id=(mirror, t), device_id_type=MESH
    )
    fwd_move = pltpu.make_async_remote_copy(
        src_ref=norm_v, dst_ref=fwd_ref.at[0], send_sem=fwd_send, recv_sem=fwd_recv, device_id=(p + 1, t), device_id_type=MESH
    )

    def sum_moves(which, buffer, sends, recvs):
        return [
            pltpu.make_async_remote_copy(
                src_ref=sum_v.at[which], dst_ref=buffer.at[d - 1], send_sem=sends.at[d - 1], recv_sem=recvs.at[d - 1],
                device_id=(p, lax.rem(t + d, members)), device_id_type=MESH,
            )
            for d in range(1, members)
        ]

    def choose(h):
        loads[h].wait()
        for i in range(3):
            send_v[h, i] = jnp.where(slot == 1, held_v[h, 1, i], held_v[h, 0, i])

    slot_load.wait()
    slot = slot_ref[mirror]
    for h in range(1):
        choose(h)
    def enter():
        pl.semaphore_wait(barrier, members + one(paired))
        for h in range(1):
            pl.when(paired)(stash[h].start)
        pl.when(has_up)(lambda: vouch(down_ready, mirror))
        pl.when(paired)(lambda: vouch(up_ready, target))

    def vouch(sem, section):
        pl.semaphore_signal(sem, inc=1, device_id=(section, t), device_id_type=MESH)

    pl.when(late)(enter)

    rows = lax.broadcasted_iota(jnp.int32, (HS, HS), 0)
    causal = rows >= lax.broadcasted_iota(jnp.int32, (HS, HS), 1)
    qkv_load.wait()
    gain_load.wait()
    squares = jnp.zeros((HS, HS), F32)
    for h in range(heads):
        cols = pl.ds(h * HS, HS)
        probs = softmax_rows(qkv_v[0, :, cols], qkv_v[1, :, cols], causal)
        out = dot(probs.astype(BF16), qkv_v[2, :, cols], ((1,), (0,))).astype(BF16)
        att_v[:, cols] = out
        out = out.astype(F32)
        squares += out * out
    sum_v[0] = jnp.broadcast_to(as_row(squares), (8, HS))
    pl.when(early)(enter)
    now_moves = sum_moves(0, sums_now, now_send, now_recv)
    for move in now_moves:
        move.start()
    window = 2
    for h in range(1, heads):
        choose(h)
    for h in range(1, window):
        pl.when(paired)(stash[h].start)


    @pl.when(to_self)
    def _():
        own = pltpu.make_async_copy(send_v, back_v, self_sem)
        own.start()
        own.wait()

    @pl.when(p == last)
    def _():
        back_v[...] = jnp.zeros_like(back_v)
        cot_v[...] = jnp.zeros_like(cot_v)

    for move in now_moves:
        move.wait_recv()
    total = sum_v[0, 0:1]
    for d in range(members - 1):
        total += sums_now[d, 0:1]
    ratio = as_columns(lax.rsqrt(total / feats + EPS))
    for h in range(heads):
        cols = pl.ds(h * HS, HS)
        norm_v[:, cols] = (att_v[:, cols].astype(F32) * ratio * gain_ref[cols][None, :]).astype(BF16)
    pl.when(paired)(lambda: pl.semaphore_wait(up_ready, 1))
    pl.when(has_up)(fwd_move.start)

    @pl.when(p == 0)
    def _():
        grad_v[0] = jnp.zeros_like(grad_v[0])
        zeros = pltpu.make_async_copy(grad_v.at[0], fwd_ref.at[0], zero_sem)
        zeros.start()
        zeros.wait()

    for h in range(window, heads):
        if h == 3:
            pl.when(has_down)(lambda: pl.semaphore_wait(down_ready, 1))
            pl.when(has_down)(cot_move.start)
        pl.when(paired)(stash[h - window].wait_send)
        pl.when(paired)(stash[h].start)
    pl.when(at_once)(evict_move.start)

    def scaled_cot(h):
        cols = pl.ds(h * HS, HS)
        return gain_ref[cols][None, :] * cot_v[:, cols].astype(F32)

    def prepare(h):
        probs = prob_v[h]
        rest = scaled_cot(h)
        d_probs = jnp.zeros((HS, HS), F32)
        for _ in range(3):
            piece = rest.astype(BF16)
            rest = rest - piece.astype(F32)
            d_probs += dot(piece, back_v[h, 2], ((1,), (1,)))
        part_v[h, 0] = probs * (d_probs - jnp.sum(probs * d_probs, axis=-1, keepdims=True)) * HS ** (-0.5)
        d_probs = dot(ob_v[h], back_v[h, 2], ((1,), (1,)))
        part_v[h, 1] = probs * (d_probs - jnp.sum(probs * d_probs, axis=-1, keepdims=True)) * HS ** (-0.5)

    pl.when(has_up)(cot_move.wait_recv)
    squares = jnp.zeros((HS, HS), F32)
    dots = jnp.zeros((HS, HS), F32)
    for h in range(heads):
        cols = pl.ds(h * HS, HS)
        if h == heads - 1:
            for move in stash[heads - window:]:
                pl.when(paired & behind)(move.wait_send)
        if h == heads - 1:
            pl.when(behind)(evict_move.start)
        pl.when(paired)(stash[h].wait_recv)
        probs = softmax_rows(back_v[h, 0], back_v[h, 1], causal)
        prob_v[h] = probs
        probs = probs.astype(BF16)
        pb_v[h] = probs
        out = dot(probs, back_v[h, 2], ((1,), (0,))).astype(BF16)
        ob_v[h] = out
        out = out.astype(F32)
        squares += out * out
        dots += scaled_cot(h) * out
        if h < heads - 1:
            prepare(h)
    sum_v[1] = jnp.concatenate([as_row(squares), as_row(dots), jnp.zeros((6, HS), F32)], axis=0)
    back_moves = sum_moves(1, sums_back, bsum_send, bsum_recv)
    for move in back_moves:
        move.start()
    pl.when(jnp.logical_not(at_once | behind))(evict_move.start)
    prepare(heads - 1)
    for move in back_moves:
        move.wait_recv()
    total = sum_v[1]
    for d in range(members - 1):
        total += sums_back[d]
    back_ratio = lax.rsqrt(total[0:1] / feats + EPS)
    pull = as_columns(back_ratio**3 * total[1:2] / feats)
    back_ratio = as_columns(back_ratio)

    grad_moves = []
    for h in range(heads):
        cols = pl.ds(h * HS, HS)
        d_out = (back_ratio * scaled_cot(h) - ob_v[h].astype(F32) * pull).astype(BF16)
        d_scores = (back_ratio * part_v[h, 0] - pull * part_v[h, 1]).astype(BF16)
        grad_v[0, :, cols] = dot(d_scores, back_v[h, 1], ((1,), (0,))).astype(BF16)
        grad_v[1, :, cols] = dot(d_scores, back_v[h, 0], ((0,), (0,))).astype(BF16)
        grad_v[2, :, cols] = dot(pb_v[h], d_out, ((0,), (0,))).astype(BF16)
        grad_moves.append(pltpu.make_async_copy(grad_v.at[:, :, cols], grads_ref.at[0, :, :, cols], grad_sem.at[h]))
        grad_moves[h].start()

    pl.when(has_down)(cot_move.wait_send)
    pl.when(has_up)(fwd_move.wait_send)
    pl.when(has_down)(fwd_move.wait_recv)
    for move in now_moves + back_moves:
        move.wait_send()
    for move in stash[heads - window:]:
        pl.when(paired & jnp.logical_not(behind))(move.wait_send)
    for move in grad_moves:
        move.wait()
    evict_move.wait()


def hand_over(fwd_in, grads_in, evict_in, fwd_out, grads_out, evict_out, sems):
    moves = [
        pltpu.make_async_copy(fwd_in, fwd_out, sems.at[0]),
        pltpu.make_async_copy(grads_in, grads_out, sems.at[1]),
        pltpu.make_async_copy(evict_in, evict_out, sems.at[2]),
    ]
    for move in moves:
        move.start()
    for move in moves:
        move.wait()


def shards(sections, members, qkv_now, held_stash, cotangent, norm_gain, fetch_slot):
    rows, width = cotangent.shape[1:]
    heads = width // HS
    anywhere = pl.BlockSpec(memory_space=pl.ANY)
    dma = pltpu.SemaphoreType.DMA
    in_hbm = functools.partial(pltpu.with_memory_space_constraint, memory_space=pltpu.HBM)
    results = pl.pallas_call(
        functools.partial(kernel, sections, members, heads, float(width * members)),
        name="section_step",
        out_shape=(
            pltpu.VMEM((1, rows, width), BF16),
            pltpu.VMEM((1, 3, rows, width), BF16),
            pltpu.VMEM((1, rows, width), BF16),
        ),
        in_specs=[anywhere] * 5,
        out_specs=(anywhere, anywhere, anywhere),
        scratch_shapes=[
            pltpu.VMEM((heads, 2, 3, rows, HS), BF16),
            pltpu.VMEM((heads, 3, rows, HS), BF16),
            pltpu.VMEM((heads, 3, rows, HS), BF16),
            pltpu.VMEM((3, rows, width), BF16),
            pltpu.VMEM((rows, width), BF16),
            pltpu.VMEM((rows, width), BF16),
            pltpu.VMEM((rows, width), BF16),
            pltpu.VMEM((heads, rows, rows), F32),
            pltpu.VMEM((heads, rows, rows), BF16),
            pltpu.VMEM((heads, rows, HS), BF16),
            pltpu.VMEM((3, rows, width), BF16),
            pltpu.VMEM((heads, 2, rows, rows), F32),
            pltpu.VMEM((2, 8, rows), F32),
            pltpu.VMEM((members - 1, 8, rows), F32),
            pltpu.VMEM((members - 1, 8, rows), F32),
            pltpu.VMEM((width,), F32),
            pltpu.SMEM((sections,), jnp.int32),
            dma, dma, dma((heads,)), dma, dma, dma, dma((heads,)),
            dma((heads,)), dma((heads,)), dma, dma, dma, dma, dma, dma,
            dma((members - 1,)), dma((members - 1,)), dma((members - 1,)), dma((members - 1,)),
            pltpu.SemaphoreType.REGULAR, pltpu.SemaphoreType.REGULAR,
        ],
        compiler_params=pltpu.CompilerParams(collective_id=0, has_side_effects=True, vmem_limit_bytes=24 * 1024 * 1024),
    )(in_hbm(qkv_now), in_hbm(held_stash), in_hbm(cotangent), in_hbm(norm_gain), in_hbm(fetch_slot))
    return pl.pallas_call(
        hand_over,
        name="hand_over",
        out_shape=tuple(pltpu.HBM(r.shape, r.dtype) for r in results),
        in_specs=[pl.BlockSpec(memory_space=pltpu.VMEM)] * 3,
        out_specs=(anywhere,) * 3,
        scratch_shapes=[dma((3,))],
    )(*[pltpu.with_memory_space_constraint(r, memory_space=pltpu.VMEM) for r in results])


def solution(mesh):
    return jax.shard_map(
        functools.partial(shards, mesh.shape["pipe"], mesh.shape["tensor"]),
        mesh=mesh,
        in_specs=(
            P("pipe", None, None, "tensor"),
            P("pipe", None, None, None, "tensor"),
            P("pipe", None, "tensor"),
            P("tensor"),
            P(),
        ),
        out_specs=(
            P("pipe", None, "tensor"),
            P("pipe", None, None, "tensor"),
            P("pipe", None, "tensor"),
        ),
        check_vma=False,
    )
```
